256 devices in a mesh: dp: 32 (over z, x), replica: 8 (over y, core).
Axes of the slice: x: 4, y: 4, z: 8, core: 2. Of those that a mesh axis runs over, the one named last changes fastest.
Arguments:
- activations: bfloat16 [114688, 8192], P(('dp', 'replica')), may hold values from -24 to 24
- out_grads: bfloat16 [114688, 256], P(('dp', 'replica')), may hold values from -0.046875 to 0.046875
- master: float32 [8192, 256], P(('dp', 'replica')), may hold values from -6 to 6
- first_moment: float32 [8192, 256], P(('dp', 'replica')), may hold values from -6 to 6
- second_moment: float32 [8192, 256], P(('dp', 'replica')), may hold values from 0.5 to 2
Outputs:
- grad_total: float32 [8192, 256], P(('dp', 'replica'))
- new_master: float32 [8192, 256], P(('dp', 'replica'))
- new_first: float32 [8192, 256], P(('dp', 'replica'))
- new_second: float32 [8192, 256], P(('dp', 'replica'))
- weights: bfloat16 [8192, 256], replicated
The draws below stay inside these ranges and needn't reach their ends.
All inputs are finite; a program needn't handle non-finite values.
Results may differ from the reference program's by a relative error of at most 0.0095.
Values may be sent and summed in bfloat16 or wider, within the bound.
A program may use at most 64 MiB of HBM per device.

```python
import math
import jax
import jax.numpy as jnp
from jax import lax

D = 8192
COLS = 256
TOK_DEV = 448
TOKENS = 114688
N_DP = 32
N_REPLICA = 8


def strengthened(entries, key, source, target, parts, factor):
    def block_of(position):
        return (jnp.arange(entries.shape[position]) // (entries.shape[position] // parts)).reshape((-1,) + (1,) * (entries.ndim - 1 - position))

    one_side = jax.random.permutation(key, parts)[block_of(target)]
    far = (block_of(target) + parts // 2) % parts
    return jnp.where((block_of(source) == one_side) | (block_of(source) == far), factor * entries, entries)


def block_scale(stream_key, extent, cuts, smallest, top_value):
    loudness, own = 1.0, jax.random.fold_in(stream_key, 6)
    for axis_at, parts in cuts:
        draws = jnp.exp(jax.random.uniform(jax.random.fold_in(own, axis_at), (parts,), jnp.float32, smallest / len(cuts), top_value / len(cuts)))
        loudness = loudness * jnp.repeat(draws, extent[axis_at] // parts).reshape([-1 if axis == axis_at else 1 for axis in range(len(extent))])
    return loudness


def gaussian(rng, shape, spread, reach, shards=(), held_as=jnp.bfloat16):
    result = jax.random.normal(rng, shape, jnp.float32) * spread
    if len(shards) > 0:
        result = block_scale(rng, shape, shards, -0.22, 0.18) * result
    return jnp.clip(result, min=-reach, max=reach).astype(held_as)


def bell_draw_with(stream_key, extent, scale, reach, pieces, heavy, kind=jnp.bfloat16):
    array = scale * jax.random.normal(stream_key, extent, jnp.float32)
    if pieces:
        array = array * block_scale(stream_key, extent, pieces, -0.22, 0.18)
    return jnp.clip(strengthened(array, jax.random.fold_in(stream_key, 3), *heavy), -reach, reach).astype(kind)


def setup_inputs(seed: int = 0) -> dict:
    key_of = jax.random.split(jax.random.key(seed), 6)
    activations = bell_draw_with(key_of[0], (TOKENS, D), 1.0, 24.0, ((0, 256),), (0, 1, 256, 6.0))
    out_grads = gaussian(key_of[1], (TOKENS, COLS), (TOKENS ** -0.5), 0.046875, ((0, 256),))
    master = gaussian(key_of[2], (D, COLS), 1.0, 6.0, ((0, 256),), jnp.float32)
    first_moment = gaussian(key_of[3], (D, COLS), 1.0, 6.0, ((0, 256),), jnp.float32)
    second_moment = jnp.clip(jnp.exp(math.log(2.0) - 1.3862944 * jax.random.uniform(key_of[4], (D, COLS), jnp.float32) ** block_scale(key_of[4], (D, COLS), ((0, 256),), -0.2, 0.2)), 0.5, 2.0)
    return dict(activations=activations, out_grads=out_grads, master=master, first_moment=first_moment, second_moment=second_moment)


beta_first = 0.9
beta_second = 0.999
learn_rate = 0.2
decay_rate = 0.1
adam_eps = 1e-08
step_count = 100

def reference(activations, out_grads, master, first_moment, second_moment):
    groups = N_DP * N_REPLICA
    act_blocks = activations.reshape(groups, TOK_DEV, D)
    grad_blocks = out_grads.reshape(groups, TOK_DEV, COLS)

    def add_code(total, pair):
        term = jnp.dot(pair[0].T, pair[1], preferred_element_type=jnp.float32)
        code = lax.optimization_barrier(term.astype(jnp.bfloat16))
        return (total + code.astype(jnp.float32), None)
    grad_total, unused = lax.scan(add_code, jnp.zeros((D, COLS), jnp.float32), (act_blocks, grad_blocks))
    new_first = beta_first * first_moment + (1.0 - beta_first) * grad_total
    new_second = beta_second * second_moment + (1.0 - beta_second) * grad_total * grad_total
    first_hat = new_first / (1.0 - beta_first ** step_count)
    second_hat = new_second / (1.0 - beta_second ** step_count)
    new_master = master - learn_rate * (first_hat / (jnp.sqrt(second_hat) + adam_eps) + decay_rate * master)
    return (grad_total, new_master, new_first, new_second, new_master.astype(jnp.bfloat16))
```

```python
import jax
import jax.numpy as jnp
from jax import lax
from jax.experimental import pallas as pl
from jax.experimental.pallas import tpu as pltpu
from jax.sharding import PartitionSpec as P

beta_first = 0.9
beta_second = 0.999
learn_rate = 0.2
decay_rate = 0.1
adam_eps = 1e-08
step_count = 100

MESH = pl.DeviceIdType.MESH
NX, NY, NZ = 4, 4, 8
TOK, D, COLS = 448, 8192, 256
CHUNK = D // NZ
ROWS = 32
HALF = COLS // 2


def kernel(a_hbm, g_hbm, master_hbm, first_hbm, second_hbm, state_ref, w_ref,
           g_ref, moments, abuf, code, sib, pair, got1, part1, got2, part2, got3,
           a_sem, in_sem, send_sem, sib_sem, rs1_sem, rs2_sem, rs3_sem, ag3_sem, ag2_sem, ag1_sem, agc_sem):
    dp, rep = lax.axis_index("dp"), lax.axis_index("replica")
    x, z, y, c = dp % NX, dp // NX, rep // 2, rep % 2
    bf16, f32 = jnp.bfloat16, jnp.float32

    def at(x, y, z, c):
        return (z * NX + x, y * 2 + c)

    def along_x(d):
        return (x + d) % NX

    def along_y(d):
        return (y + d) % NY

    def along_z(d):
        return (z + d) % NZ

    def z_shift(i):
        return jnp.where(i % 2 == 0, 4 + i // 2, (7 - i) // 2)

    def fetch(i):
        begin = pl.multiple_of(along_z(z_shift(i)) * CHUNK, CHUNK)
        return pltpu.make_async_copy(a_hbm.at[:, pl.ds(begin, CHUNK)], abuf.at[i], a_sem.at[i])

    def send(src, dst, stage, sem, target):
        return pltpu.make_async_remote_copy(
            src_ref=src, dst_ref=dst, send_sem=send_sem.at[stage], recv_sem=sem,
            device_id=target, device_id_type=MESH)

    def each(n, f, start=0):
        def step(i, carry):
            f(i)
            return carry
        lax.fori_loop(start, n, step, 0)

    def arrived(ref, sem):
        pltpu.make_async_remote_copy(
            src_ref=ref, dst_ref=ref, send_sem=send_sem.at[0], recv_sem=sem,
            device_id=at(x, y, z, 1 - c), device_id_type=MESH).wait_recv()

    def left(ref, stage):
        pltpu.make_async_remote_copy(
            src_ref=ref, dst_ref=ref, send_sem=send_sem.at[stage], recv_sem=sib_sem.at[0],
            device_id=at(x, y, z, 1 - c), device_id_type=MESH).wait_send()

    barrier = pltpu.get_barrier_semaphore()
    peers = [at(x, y, z, 1 - c)]
    peers += [at(along_x(d), y, z, c) for d in range(1, NX)]
    peers += [at(x, along_y(d), z, c) for d in range(1, NY)]
    peers += [at(x, y, along_z(d), c) for d in range(1, NZ)]
    for peer in peers:
        pl.semaphore_signal(barrier, inc=1, device_id=peer, device_id_type=MESH)
    loads = [pltpu.make_async_copy(g_hbm, g_ref, in_sem.at[0])]
    for i, ref in enumerate((master_hbm, first_hbm, second_hbm)):
        loads.append(pltpu.make_async_copy(ref, moments.at[i], in_sem.at[1 + i]))
    loads[0].start()
    each(NZ, lambda i: fetch(i).start())
    for load in loads[1:]:
        load.start()
    loads[0].wait()

    def multiply(i):
        fetch(i).wait()
        term = lax.dot_general(abuf[i], g_ref[...], (((0,), (0,)), ((), ())), preferred_element_type=f32)
        code[i] = term.astype(bf16).reshape(NX, NY, 2, ROWS, COLS)

    def send_sib(i):
        send(code.at[i, :, :, 1 - c], sib.at[i], 0, sib_sem.at[i], at(x, y, z, 1 - c)).start()

    def add_pair(i):
        arrived(sib.at[i], sib_sem.at[i])
        pair[i] = (code[i, :, :, c].astype(f32) + sib[i].astype(f32)).astype(bf16)

    def send_1(i):
        for d in (2, 1, 3):
            send(pair.at[i, along_x(d), :, :, pl.ds(0, HALF)], got1.at[i, d - 1], 1, rs1_sem.at[i],
                 at(along_x(d), y, z, c)).start()
            send(pair.at[i, :, along_y(d), :, pl.ds(HALF, HALF)], got1.at[i, 2 + d], 1, rs1_sem.at[i],
                 at(x, along_y(d), z, c)).start()

    def add_1(i):
        arrived(got1.at[i], rs1_sem.at[i])
        p = pair[i, x, :, :, 0:HALF].astype(f32)
        q = pair[i, :, y, :, HALF:COLS].astype(f32)
        for d in range(3):
            p = p + got1[i, d].astype(f32)
            q = q + got1[i, 3 + d].astype(f32)
        part1[i, 0] = p.astype(bf16)
        part1[i, 1] = q.astype(bf16)

    def send_2(i):
        for d in (2, 1, 3):
            send(part1.at[i, 0, along_y(d)], got2.at[i, d - 1], 2, rs2_sem.at[i], at(x, along_y(d), z, c)).start()
            send(part1.at[i, 1, along_x(d)], got2.at[i, 2 + d], 2, rs2_sem.at[i], at(along_x(d), y, z, c)).start()

    def add_2(i):
        arrived(got2.at[i], rs2_sem.at[i])
        p = part1[i, 0, y].astype(f32)
        q = part1[i, 1, x].astype(f32)
        for d in range(3):
            p = p + got2[i, d].astype(f32)
            q = q + got2[i, 3 + d].astype(f32)
        part2[i, :, 0:HALF] = p
        part2[i, :, HALF:COLS] = q

    def send_3(i):
        send(part2.at[i], got3.at[i], 3, rs3_sem.at[i], at(x, y, along_z(z_shift(i)), c)).start()

    multiply(0)
    pl.semaphore_wait(barrier, len(peers))
    send_sib(0)

    def phase_a(i):
        multiply(i)
        send_sib(i)

        @pl.when(i >= 2)
        def _():
            add_pair(i - 2)
            send_1(i - 2)
    each(NZ, phase_a, 1)

    def phase_a_end(i):
        add_pair(i)
        send_1(i)
    each(NZ, phase_a_end, NZ - 2)

    def phase_b(i):
        add_1(i)
        send_2(i)

        @pl.when(i >= 2)
        def _():
            add_2(i - 2)
            send_3(i - 2)
    each(NZ, phase_b)
    add_2(NZ - 2)
    send_3(NZ - 2)
    add_2(NZ - 1)

    for load in loads[1:]:
        load.wait()
    grad = part2[NZ - 1]
    for i in range(NZ - 1):
        arrived(got3.at[i], rs3_sem.at[i])
        grad = grad + got3[i]
    new_first = beta_first * moments[1] + (1.0 - beta_first) * grad
    new_second = beta_second * moments[2] + (1.0 - beta_second) * grad * grad
    first_hat = new_first / (1.0 - beta_first**step_count)
    second_hat = new_second / (1.0 - beta_second**step_count)
    master = moments[0]
    new_master = master - learn_rate * (
        first_hat / (jnp.sqrt(second_hat) + adam_eps) + decay_rate * master
    )
    w_ref[z, x, y, c] = new_master.astype(bf16)

    def gather_3(i):
        mine = w_ref.at[z, x, y, c]
        send(mine, mine, 4, ag3_sem.at[i], at(x, y, along_z(z_shift(i)), c)).start()
    each(NZ - 1, gather_3)
    state_ref[0] = grad
    state_ref[1] = new_master
    state_ref[2] = new_first
    state_ref[3] = new_second

    def z_of(j):
        return along_z(z_shift(NZ - 1 - j))

    def gather_2(j):
        @pl.when(j >= 1)
        def _():
            shift = (NZ - z_shift(NZ - 1 - j)) % NZ
            slot = jnp.where(shift >= 4, 2 * (shift - 4), 7 - 2 * shift)
            arrived(w_ref.at[0, 0, 0, 0], ag3_sem.at[slot])
        k = z_of(j)
        p = w_ref.at[k, x, y, c, :, pl.ds(0, HALF)]
        q = w_ref.at[k, x, y, c, :, pl.ds(HALF, HALF)]
        for d in (2, 1, 3):
            send(p, p, 5, ag2_sem.at[j], at(x, along_y(d), z, c)).start()
            send(q, q, 5, ag2_sem.at[j], at(along_x(d), y, z, c)).start()

    def gather_1(j):
        arrived(got2.at[0], ag2_sem.at[j])
        k = z_of(j)
        p = w_ref.at[k, x, :, c, :, pl.ds(0, HALF)]
        q = w_ref.at[k, :, y, c, :, pl.ds(HALF, HALF)]
        for d in (2, 1, 3):
            send(p, p, 6, ag1_sem.at[j], at(along_x(d), y, z, c)).start()
            send(q, q, 6, ag1_sem.at[j], at(x, along_y(d), z, c)).start()

    def gather_c(j):
        arrived(got1.at[0], ag1_sem.at[j])
        k = z_of(j)
        whole = w_ref.at[k, :, :, c]
        send(whole, whole, 7, agc_sem.at[j], at(x, y, z, 1 - c)).start()

    def phase_c(j):
        @pl.when(j < NZ)
        def _():
            gather_2(j)

        @pl.when((j >= 1) & (j < NZ + 1))
        def _():
            gather_1(j - 1)

        @pl.when(j >= 4)
        def _():
            gather_c(j - 4)
    each(NZ + 4, phase_c)

    each(NZ, lambda j: arrived(sib.at[0], agc_sem.at[j]))
    left(sib, 0)
    left(got1, 1)
    left(got2, 2)
    left(got3, 3)
    each(NZ - 1, lambda i: left(w_ref.at[0, 0, 0, 0], 4))
    left(got2, 5)
    left(got1, 6)
    left(sib, 7)


def finish(state_ref, w_ref, grad_ref, master_ref, first_ref, second_ref, out_ref, sem):
    copies = [pltpu.make_async_copy(w_ref, out_ref, sem.at[4])]
    for i, ref in enumerate((grad_ref, master_ref, first_ref, second_ref)):
        copies.append(pltpu.make_async_copy(state_ref.at[i], ref, sem.at[i]))
    for copy in copies:
        copy.start()
    for copy in copies:
        copy.wait()


def body(activations, out_grads, master, first_moment, second_moment):
    f32, bf16 = jnp.float32, jnp.bfloat16
    vmem = pl.BlockSpec(memory_space=pltpu.VMEM)
    anywhere = pl.BlockSpec(memory_space=pl.ANY)
    dma = pltpu.SemaphoreType.DMA
    state, w = pl.pallas_call(
        kernel,
        name="reduce_update_gather",
        out_shape=(
            pltpu.VMEM((4, ROWS, COLS), f32),
            pltpu.VMEM((NZ, NX, NY, 2, ROWS, COLS), bf16),
        ),
        in_specs=[anywhere] * 5,
        out_specs=(vmem, vmem),
        scratch_shapes=[
            pltpu.VMEM((TOK, COLS), bf16),
            pltpu.VMEM((3, ROWS, COLS), f32),
            pltpu.VMEM((NZ, TOK, CHUNK), bf16),
            pltpu.VMEM((NZ, NX, NY, 2, ROWS, COLS), bf16),
            pltpu.VMEM((NZ, NX, NY, ROWS, COLS), bf16),
            pltpu.VMEM((NZ, NX, NY, ROWS, COLS), bf16),
            pltpu.VMEM((NZ, 6, 4, ROWS, HALF), bf16),
            pltpu.VMEM((NZ, 2, 4, ROWS, HALF), bf16),
            pltpu.VMEM((NZ, 6, ROWS, HALF), bf16),
            pltpu.VMEM((NZ, ROWS, COLS), f32),
            pltpu.VMEM((NZ - 1, ROWS, COLS), f32),
            dma((NZ,)), dma((4,)), dma((8,)),
            dma((NZ,)), dma((NZ,)), dma((NZ,)), dma((NZ,)),
            dma((NZ,)), dma((NZ,)), dma((NZ,)), dma((NZ,)),
        ],
        compiler_params=pltpu.CompilerParams(
            collective_id=0, has_side_effects=True, vmem_limit_bytes=58 << 20
        ),
    )(activations, out_grads, master, first_moment, second_moment)
    row = jax.ShapeDtypeStruct((ROWS, COLS), f32)
    out = pl.pallas_call(
        finish,
        name="write_out",
        out_shape=(row, row, row, row, jax.ShapeDtypeStruct((NZ, NX, NY, 2, ROWS, COLS), bf16)),
        in_specs=[anywhere, anywhere],
        out_specs=(anywhere,) * 5,
        scratch_shapes=[dma((5,))],
        compiler_params=pltpu.CompilerParams(vmem_limit_bytes=1 << 20),
    )(state, w)
    return out[:4] + (out[4].reshape(D, COLS),)


def solution(mesh):
    spec = P(("dp", "replica"), None)
    return jax.shard_map(
        body, mesh=mesh, in_specs=(spec,) * 5, out_specs=(spec,) * 4 + (P(),), check_vma=False
    )
```

```python
import jax
import jax.numpy as jnp
from jax import lax
from jax.experimental import pallas as pl
from jax.experimental.pallas import tpu as pltpu
from jax.sharding import PartitionSpec as P

beta_first = 0.9
beta_second = 0.999
learn_rate = 0.2
decay_rate = 0.1
adam_eps = 1e-08
step_count = 100

MESH = pl.DeviceIdType.MESH
NX, NY, NZ = 4, 4, 8
TOK, D, COLS = 448, 8192, 256
CHUNK = D // NZ
ROWS = 32
HALF = COLS // 2
AHEAD = 3
LAGS = (2, 5, 8, 10, 13)


def kernel(a_hbm, g_hbm, master_hbm, first_hbm, second_hbm, state_ref, w_ref,
           g_ref, moments, abuf, code, sib, pair, got1, part1, got2, part2, got3,
           a_sem, in_sem, send_sem, sib_sem, rs1_sem, rs2_sem, rs3_sem, ag3_sem, ag2_sem, ag1_sem, agc_sem):
    dp, rep = lax.axis_index("dp"), lax.axis_index("replica")
    x, z, y, c = dp % NX, dp // NX, rep // 2, rep % 2
    bf16, f32 = jnp.bfloat16, jnp.float32

    def at(x, y, z, c):
        return (z * NX + x, y * 2 + c)

    def along_x(d):
        return (x + d) % NX

    def along_y(d):
        return (y + d) % NY

    def along_z(d):
        return (z + d) % NZ

    def z_of(i):
        return 4 * (i % 2) + 2 * (i // 2 % 2) + i // 4

    def fetch(i):
        begin = pl.multiple_of(z_of(i) * CHUNK, CHUNK)
        return pltpu.make_async_copy(a_hbm.at[:, pl.ds(begin, CHUNK)], abuf.at[i], a_sem.at[i])

    def send(src, dst, stage, sem, target):
        return pltpu.make_async_remote_copy(
            src_ref=src, dst_ref=dst, send_sem=send_sem.at[stage], recv_sem=sem,
            device_id=target, device_id_type=MESH)

    def each(n, f, start=0):
        def step(i, carry):
            f(i)
            return carry
        lax.fori_loop(start, n, step, 0)

    def arrived(ref, sem):
        pltpu.make_async_remote_copy(
            src_ref=ref, dst_ref=ref, send_sem=send_sem.at[0], recv_sem=sem,
            device_id=at(x, y, z, 1 - c), device_id_type=MESH).wait_recv()

    def left(ref, stage):
        pltpu.make_async_remote_copy(
            src_ref=ref, dst_ref=ref, send_sem=send_sem.at[stage], recv_sem=sib_sem.at[0],
            device_id=at(x, y, z, 1 - c), device_id_type=MESH).wait_send()

    barrier = pltpu.get_barrier_semaphore()
    peers = [at(x, y, z, 1 - c)]
    peers += [at(along_x(d), y, z, c) for d in range(1, NX)]
    peers += [at(x, along_y(d), z, c) for d in range(1, NY)]
    peers += [at(x, y, along_z(d), c) for d in range(1, NZ)]
    for peer in peers:
        pl.semaphore_signal(barrier, inc=1, device_id=peer, device_id_type=MESH)
    loads = [pltpu.make_async_copy(g_hbm, g_ref, in_sem.at[0])]
    for i, ref in enumerate((master_hbm, first_hbm, second_hbm)):
        loads.append(pltpu.make_async_copy(ref, moments.at[i], in_sem.at[1 + i]))
    loads[0].start()
    each(NZ, lambda i: fetch(i).start())
    for load in loads[1:]:
        load.start()
    loads[0].wait()

    def multiply(i):
        fetch(i).wait()
        term = lax.dot_general(abuf[i], g_ref[...], (((0,), (0,)), ((), ())), preferred_element_type=f32)
        code[i] = term.astype(bf16).reshape(NX, NY, 2, ROWS, COLS)

    def send_sib(i):
        send(code.at[i, :, :, 1 - c], sib.at[i], 0, sib_sem.at[i], at(x, y, z, 1 - c)).start()

    def add_pair(i):
        arrived(sib.at[i], sib_sem.at[i])
        pair[i] = (code[i, :, :, c].astype(f32) + sib[i].astype(f32)).astype(bf16)

    def send_1(i):
        for d in (2, 1, 3):
            send(pair.at[i, along_x(d), :, :, pl.ds(0, HALF)], got1.at[i, d - 1], 1, rs1_sem.at[i],
                 at(along_x(d), y, z, c)).start()
            send(pair.at[i, :, along_y(d), :, pl.ds(HALF, HALF)], got1.at[i, 2 + d], 1, rs1_sem.at[i],
                 at(x, along_y(d), z, c)).start()

    def add_1(i):
        arrived(got1.at[i], rs1_sem.at[i])
        p = pair[i, x, :, :, 0:HALF].astype(f32)
        q = pair[i, :, y, :, HALF:COLS].astype(f32)
        for d in range(3):
            p = p + got1[i, d].astype(f32)
            q = q + got1[i, 3 + d].astype(f32)
        part1[i, 0] = p.astype(bf16)
        part1[i, 1] = q.astype(bf16)

    def send_2(i):
        for d in (2, 1, 3):
            send(part1.at[i, 0, along_y(d)], got2.at[i, d - 1], 2, rs2_sem.at[i], at(x, along_y(d), z, c)).start()
            send(part1.at[i, 1, along_x(d)], got2.at[i, 2 + d], 2, rs2_sem.at[i], at(along_x(d), y, z, c)).start()

    def add_2(i):
        arrived(got2.at[i], rs2_sem.at[i])
        p = part1[i, 0, y].astype(f32)
        q = part1[i, 1, x].astype(f32)
        for d in range(3):
            p = p + got2[i, d].astype(f32)
            q = q + got2[i, 3 + d].astype(f32)
        part2[i, :, 0:HALF] = p.astype(bf16)
        part2[i, :, HALF:COLS] = q.astype(bf16)

    def send_3(i):
        @pl.when(z != z_of(i))
        def _():
            slot = (z_of(i) - z + NZ - 1) % NZ
            send(part2.at[i], got3.at[slot], 3, rs3_sem.at[0], at(x, y, z_of(i), c)).start()

    def update(i):
        for load in loads[1:]:
            load.wait()
        arrived(got3, rs3_sem.at[0])
        grad = part2[i].astype(f32)
        for d in range(NZ - 1):
            grad = grad + got3[d].astype(f32)
        new_first = beta_first * moments[1] + (1.0 - beta_first) * grad
        new_second = beta_second * moments[2] + (1.0 - beta_second) * grad * grad
        first_hat = new_first / (1.0 - beta_first**step_count)
        second_hat = new_second / (1.0 - beta_second**step_count)
        master = moments[0]
        new_master = master - learn_rate * (
            first_hat / (jnp.sqrt(second_hat) + adam_eps) + decay_rate * master
        )
        w_ref[z, x, y, c] = new_master.astype(bf16)
        mine = w_ref.at[z, x, y, c]
        for d in (4, 3, 5, 2, 6, 1, 7):
            send(mine, mine, 4, ag3_sem.at[i], at(x, y, along_z(d), c)).start()
        state_ref[0] = grad
        state_ref[1] = new_master
        state_ref[2] = new_first
        state_ref[3] = new_second

    def gather_2(i):
        k = z_of(i)

        @pl.when(z != k)
        def _():
            arrived(w_ref.at[0, 0, 0, 0], ag3_sem.at[i])
        p = w_ref.at[k, x, y, c, :, pl.ds(0, HALF)]
        q = w_ref.at[k, x, y, c, :, pl.ds(HALF, HALF)]
        for d in (2, 1, 3):
            send(p, p, 5, ag2_sem.at[i], at(x, along_y(d), z, c)).start()
            send(q, q, 5, ag2_sem.at[i], at(along_x(d), y, z, c)).start()

    def gather_1(i):
        arrived(got2.at[0], ag2_sem.at[i])
        k = z_of(i)
        p = w_ref.at[k, x, :, c, :, pl.ds(0, HALF)]
        q = w_ref.at[k, :, y, c, :, pl.ds(HALF, HALF)]
        for d in (2, 1, 3):
            send(p, p, 6, ag1_sem.at[i], at(along_x(d), y, z, c)).start()
            send(q, q, 6, ag1_sem.at[i], at(x, along_y(d), z, c)).start()

    def gather_c(i):
        arrived(got1.at[0], ag1_sem.at[i])
        whole = w_ref.at[z_of(i), :, :, c]
        send(whole, whole, 7, agc_sem.at[i], at(x, y, z, 1 - c)).start()

    multiply(0)
    pl.semaphore_wait(barrier, len(peers))
    send_sib(0)

    def phase_a(i):
        multiply(i)
        send_sib(i)

        @pl.when(i >= 2)
        def _():
            add_pair(i - 2)

        @pl.when((i >= 2) & (i < AHEAD + 2))
        def _():
            send_1(i - 2)
    each(NZ, phase_a, 1)

    def phase_a_end(i):
        add_pair(i)
        pl.when(i < AHEAD)(lambda: send_1(i))
    each(NZ, phase_a_end, NZ - 2)

    def stage(s, lag, f):
        pl.when((s >= lag) & (s < lag + NZ))(lambda: f(s - lag))

    def phase_b(s):
        def sum_1(i):
            add_1(i)
            send_2(i)
            pl.when(i < NZ - AHEAD)(lambda: send_1(i + AHEAD))

        def sum_2(i):
            add_2(i)
            send_3(i)

        def own(i):
            pl.when(z == z_of(i))(lambda: update(i))
        stage(s, 0, sum_1)
        stage(s, LAGS[0], sum_2)
        stage(s, LAGS[1], own)
        stage(s, LAGS[2], gather_2)
        stage(s, LAGS[3], gather_1)
        stage(s, LAGS[4], gather_c)
    each(NZ + LAGS[4], phase_b)

    each(NZ, lambda j: arrived(sib.at[0], agc_sem.at[j]))
    left(sib, 0)
    left(got1, 1)
    left(got2, 2)
    left(got3, 3)
    each(NZ - 1, lambda i: left(w_ref.at[0, 0, 0, 0], 4))
    left(got2, 5)
    left(got1, 6)
    left(sib, 7)


def finish(state_ref, w_ref, grad_ref, master_ref, first_ref, second_ref, out_ref, sem):
    copies = [pltpu.make_async_copy(w_ref, out_ref, sem.at[4])]
    for i, ref in enumerate((grad_ref, master_ref, first_ref, second_ref)):
        copies.append(pltpu.make_async_copy(state_ref.at[i], ref, sem.at[i]))
    for copy in copies:
        copy.start()
    for copy in copies:
        copy.wait()


def body(activations, out_grads, master, first_moment, second_moment):
    f32, bf16 = jnp.float32, jnp.bfloat16
    vmem = pl.BlockSpec(memory_space=pltpu.VMEM)
    anywhere = pl.BlockSpec(memory_space=pl.ANY)
    dma = pltpu.SemaphoreType.DMA
    state, w = pl.pallas_call(
        kernel,
        name="reduce_update_gather",
        out_shape=(
            pltpu.VMEM((4, ROWS, COLS), f32),
            pltpu.VMEM((NZ, NX, NY, 2, ROWS, COLS), bf16),
        ),
        in_specs=[anywhere] * 5,
        out_specs=(vmem, vmem),
        scratch_shapes=[
            pltpu.VMEM((TOK, COLS), bf16),
            pltpu.VMEM((3, ROWS, COLS), f32),
            pltpu.VMEM((NZ, TOK, CHUNK), bf16),
            pltpu.VMEM((NZ, NX, NY, 2, ROWS, COLS), bf16),
            pltpu.VMEM((NZ, NX, NY, ROWS, COLS), bf16),
            pltpu.VMEM((NZ, NX, NY, ROWS, COLS), bf16),
            pltpu.VMEM((NZ, 6, 4, ROWS, HALF), bf16),
            pltpu.VMEM((NZ, 2, 4, ROWS, HALF), bf16),
            pltpu.VMEM((NZ, 6, ROWS, HALF), bf16),
            pltpu.VMEM((NZ, ROWS, COLS), bf16),
            pltpu.VMEM((NZ - 1, ROWS, COLS), bf16),
            dma((NZ,)), dma((4,)), dma((8,)),
            dma((NZ,)), dma((NZ,)), dma((NZ,)), dma((NZ,)),
            dma((NZ,)), dma((NZ,)), dma((NZ,)), dma((NZ,)),
        ],
        compiler_params=pltpu.CompilerParams(
            collective_id=0, has_side_effects=True, vmem_limit_bytes=58 << 20
        ),
    )(activations, out_grads, master, first_moment, second_moment)
    row = jax.ShapeDtypeStruct((ROWS, COLS), f32)
    out = pl.pallas_call(
        finish,
        name="write_out",
        out_shape=(row, row, row, row, jax.ShapeDtypeStruct((NZ, NX, NY, 2, ROWS, COLS), bf16)),
        in_specs=[anywhere, anywhere],
        out_specs=(anywhere,) * 5,
        scratch_shapes=[dma((5,))],
        compiler_params=pltpu.CompilerParams(vmem_limit_bytes=1 << 20),
    )(state, w)
    return out[:4] + (out[4].reshape(D, COLS),)


def solution(mesh):
    spec = P(("dp", "replica"), None)
    return jax.shard_map(
        body, mesh=mesh, in_specs=(spec,) * 5, out_specs=(spec,) * 4 + (P(),), check_vma=False
    )
```

```python
import jax
import jax.numpy as jnp
from jax import lax
from jax.experimental import pallas as pl
from jax.experimental.pallas import tpu as pltpu
from jax.sharding import PartitionSpec as P

beta_first = 0.9
beta_second = 0.999
learn_rate = 0.2
decay_rate = 0.1
adam_eps = 1e-08
step_count = 100

MESH = pl.DeviceIdType.MESH
NX, NY, NZ = 4, 4, 8
TOK, D, COLS = 448, 8192, 256
CHUNK = D // NZ
ROWS = 32
HALF = COLS // 2
AHEAD = 3
LAGS = (2, 5, 7, 9, 12)


def kernel(a_hbm, g_hbm, master_hbm, first_hbm, second_hbm, state_ref, w_ref,
           g_ref, moments, abuf, code, sib, pair, got1, part1, got2, part2, got3,
           a_sem, in_sem, send_sem, sib_sem, rs1_sem, rs2_sem, rs3_sem, ag3_sem, ag2_sem, ag1_sem, agc_sem):
    dp, rep = lax.axis_index("dp"), lax.axis_index("replica")
    x, z, y, c = dp % NX, dp // NX, rep // 2, rep % 2
    bf16, f32 = jnp.bfloat16, jnp.float32

    def at(x, y, z, c):
        return (z * NX + x, y * 2 + c)

    def along_x(d):
        return (x + d) % NX

    def along_y(d):
        return (y + d) % NY

    def along_z(d):
        return (z + d) % NZ

    def z_of(i):
        return 4 * (i % 2) + 2 * (i // 2 % 2) + i // 4

    def fetch(i):
        begin = pl.multiple_of(z_of(i) * CHUNK, CHUNK)
        return pltpu.make_async_copy(a_hbm.at[:, pl.ds(begin, CHUNK)], abuf.at[i], a_sem.at[i])

    def send(src, dst, stage, sem, target):
        return pltpu.make_async_remote_copy(
            src_ref=src, dst_ref=dst, send_sem=send_sem.at[stage], recv_sem=sem,
            device_id=target, device_id_type=MESH)

    def each(n, f, start=0):
        def step(i, carry):
            f(i)
            return carry
        lax.fori_loop(start, n, step, 0)

    def arrived(ref, sem):
        pltpu.make_async_remote_copy(
            src_ref=ref, dst_ref=ref, send_sem=send_sem.at[0], recv_sem=sem,
            device_id=at(x, y, z, 1 - c), device_id_type=MESH).wait_recv()

    def left(ref, stage):
        pltpu.make_async_remote_copy(
            src_ref=ref, dst_ref=ref, send_sem=send_sem.at[stage], recv_sem=sib_sem.at[0],
            device_id=at(x, y, z, 1 - c), device_id_type=MESH).wait_send()

    barrier = pltpu.get_barrier_semaphore()
    peers = [at(x, y, z, 1 - c)]
    peers += [at(along_x(d), y, z, c) for d in range(1, NX)]
    peers += [at(x, along_y(d), z, c) for d in range(1, NY)]
    peers += [at(x, y, along_z(d), c) for d in range(1, NZ)]
    for peer in peers:
        pl.semaphore_signal(barrier, inc=1, device_id=peer, device_id_type=MESH)
    loads = [pltpu.make_async_copy(g_hbm, g_ref, in_sem.at[0])]
    for i, ref in enumerate((master_hbm, first_hbm, second_hbm)):
        loads.append(pltpu.make_async_copy(ref, moments.at[i], in_sem.at[1 + i]))
    loads[0].start()
    each(NZ, lambda i: fetch(i).start())
    for load in loads[1:]:
        load.start()
    loads[0].wait()

    def multiply(i):
        fetch(i).wait()
        term = lax.dot_general(abuf[i], g_ref[...], (((0,), (0,)), ((), ())), preferred_element_type=f32)
        code[i] = term.astype(bf16).reshape(NX, NY, 2, ROWS, COLS)

    def send_sib(i):
        send(code.at[i, :, :, 1 - c], sib.at[i], 0, sib_sem.at[i], at(x, y, z, 1 - c)).start()

    def add_pair(i):
        arrived(sib.at[i], sib_sem.at[i])
        pair[i] = (code[i, :, :, c].astype(f32) + sib[i].astype(f32)).astype(bf16)

    def send_1(i):
        for d in (2, 1, 3):
            send(pair.at[i, along_x(d), :, :, pl.ds(0, HALF)], got1.at[i, d - 1], 1, rs1_sem.at[i],
                 at(along_x(d), y, z, c)).start()
            send(pair.at[i, :, along_y(d), :, pl.ds(HALF, HALF)], got1.at[i, 2 + d], 1, rs1_sem.at[i],
                 at(x, along_y(d), z, c)).start()

    def add_1(i):
        arrived(got1.at[i], rs1_sem.at[i])
        p = pair[i, x, :, :, 0:HALF].astype(f32)
        q = pair[i, :, y, :, HALF:COLS].astype(f32)
        for d in range(3):
            p = p + got1[i, d].astype(f32)
            q = q + got1[i, 3 + d].astype(f32)
        part1[i, 0] = p.astype(bf16)
        part1[i, 1] = q.astype(bf16)

    def send_2(i):
        for d in (2, 1, 3):
            send(part1.at[i, 0, along_y(d)], got2.at[i, d - 1], 2, rs2_sem.at[i], at(x, along_y(d), z, c)).start()
            send(part1.at[i, 1, along_x(d)], got2.at[i, 2 + d], 2, rs2_sem.at[i], at(along_x(d), y, z, c)).start()

    def add_2(i):
        arrived(got2.at[i], rs2_sem.at[i])
        p = part1[i, 0, y].astype(f32)
        q = part1[i, 1, x].astype(f32)
        for d in range(3):
            p = p + got2[i, d].astype(f32)
            q = q + got2[i, 3 + d].astype(f32)
        part2[i, :, 0:HALF] = p.astype(bf16)
        part2[i, :, HALF:COLS] = q.astype(bf16)

    def send_3(i):
        @pl.when(z != z_of(i))
        def _():
            slot = (z_of(i) - z + NZ - 1) % NZ
            send(part2.at[i], got3.at[slot], 3, rs3_sem.at[0], at(x, y, z_of(i), c)).start()

    def update(i):
        for load in loads[1:]:
            load.wait()
        arrived(got3, rs3_sem.at[0])
        grad = part2[i].astype(f32)
        for d in range(NZ - 1):
            grad = grad + got3[d].astype(f32)
        new_first = beta_first * moments[1] + (1.0 - beta_first) * grad
        new_second = beta_second * moments[2] + (1.0 - beta_second) * grad * grad
        first_hat = new_first / (1.0 - beta_first**step_count)
        second_hat = new_second / (1.0 - beta_second**step_count)
        master = moments[0]
        new_master = master - learn_rate * (
            first_hat / (jnp.sqrt(second_hat) + adam_eps) + decay_rate * master
        )
        w_ref[z, x, y, c] = new_master.astype(bf16)
        mine = w_ref.at[z, x, y, c]
        for d in (4, 3, 5, 2, 6, 1, 7):
            send(mine, mine, 4, ag3_sem.at[i], at(x, y, along_z(d), c)).start()
        state_ref[0] = grad
        state_ref[1] = new_master
        state_ref[2] = new_first
        state_ref[3] = new_second

    def gather_2(i):
        k = z_of(i)

        @pl.when(z != k)
        def _():
            arrived(w_ref.at[0, 0, 0, 0], ag3_sem.at[i])
        p = w_ref.at[k, x, y, c, :, pl.ds(0, HALF)]
        q = w_ref.at[k, x, y, c, :, pl.ds(HALF, HALF)]
        for d in (2, 1, 3):
            send(p, p, 5, ag2_sem.at[i], at(x, along_y(d), z, c)).start()
            send(q, q, 5, ag2_sem.at[i], at(along_x(d), y, z, c)).start()

    def gather_1(i):
        arrived(got2.at[0], ag2_sem.at[i])
        k = z_of(i)
        p = w_ref.at[k, x, :, c, :, pl.ds(0, HALF)]
        q = w_ref.at[k, :, y, c, :, pl.ds(HALF, HALF)]
        for d in (2, 1, 3):
            send(p, p, 6, ag1_sem.at[i], at(along_x(d), y, z, c)).start()
            send(q, q, 6, ag1_sem.at[i], at(x, along_y(d), z, c)).start()

    def gather_c(i):
        arrived(got1.at[0], ag1_sem.at[i])
        whole = w_ref.at[z_of(i), :, :, c]
        send(whole, whole, 7, agc_sem.at[i], at(x, y, z, 1 - c)).start()

    multiply(0)
    pl.semaphore_wait(barrier, len(peers))
    send_sib(0)

    def phase_a(i):
        multiply(i)
        send_sib(i)

        @pl.when(i >= 3)
        def _():
            add_pair(i - 3)

        @pl.when((i >= 3) & (i < AHEAD + 3))
        def _():
            send_1(i - 3)
    each(NZ, phase_a, 1)

    def phase_a_end(i):
        add_pair(i)
        pl.when(i < AHEAD)(lambda: send_1(i))
    each(NZ, phase_a_end, NZ - 3)

    def stage(s, lag, f):
        pl.when((s >= lag) & (s < lag + NZ))(lambda: f(s - lag))

    def phase_b(s):
        def sum_1(i):
            add_1(i)
            send_2(i)
            pl.when(i < NZ - AHEAD)(lambda: send_1(i + AHEAD))

        def sum_2(i):
            add_2(i)
            send_3(i)

        def own(i):
            pl.when(z == z_of(i))(lambda: update(i))
        stage(s, 0, sum_1)
        stage(s, LAGS[0], sum_2)
        stage(s, LAGS[1], own)
        stage(s, LAGS[2], gather_2)
        stage(s, LAGS[3], gather_1)
        stage(s, LAGS[4], gather_c)
    each(NZ + LAGS[4], phase_b)

    each(NZ, lambda j: arrived(sib.at[0], agc_sem.at[j]))
    left(sib, 0)
    left(got1, 1)
    left(got2, 2)
    left(got3, 3)
    each(NZ - 1, lambda i: left(w_ref.at[0, 0, 0, 0], 4))
    left(got2, 5)
    left(got1, 6)
    left(sib, 7)


def finish(state_ref, w_ref, grad_ref, master_ref, first_ref, second_ref, out_ref, sem):
    copies = [pltpu.make_async_copy(w_ref, out_ref, sem.at[4])]
    for i, ref in enumerate((grad_ref, master_ref, first_ref, second_ref)):
        copies.append(pltpu.make_async_copy(state_ref.at[i], ref, sem.at[i]))
    for copy in copies:
        copy.start()
    for copy in copies:
        copy.wait()


def body(activations, out_grads, master, first_moment, second_moment):
    f32, bf16 = jnp.float32, jnp.bfloat16
    vmem = pl.BlockSpec(memory_space=pltpu.VMEM)
    anywhere = pl.BlockSpec(memory_space=pl.ANY)
    dma = pltpu.SemaphoreType.DMA
    state, w = pl.pallas_call(
        kernel,
        name="reduce_update_gather",
        out_shape=(
            pltpu.VMEM((4, ROWS, COLS), f32),
            pltpu.VMEM((NZ, NX, NY, 2, ROWS, COLS), bf16),
        ),
        in_specs=[anywhere] * 5,
        out_specs=(vmem, vmem),
        scratch_shapes=[
            pltpu.VMEM((TOK, COLS), bf16),
            pltpu.VMEM((3, ROWS, COLS), f32),
            pltpu.VMEM((NZ, TOK, CHUNK), bf16),
            pltpu.VMEM((NZ, NX, NY, 2, ROWS, COLS), bf16),
            pltpu.VMEM((NZ, NX, NY, ROWS, COLS), bf16),
            pltpu.VMEM((NZ, NX, NY, ROWS, COLS), bf16),
            pltpu.VMEM((NZ, 6, 4, ROWS, HALF), bf16),
            pltpu.VMEM((NZ, 2, 4, ROWS, HALF), bf16),
            pltpu.VMEM((NZ, 6, ROWS, HALF), bf16),
            pltpu.VMEM((NZ, ROWS, COLS), bf16),
            pltpu.VMEM((NZ - 1, ROWS, COLS), bf16),
            dma((NZ,)), dma((4,)), dma((8,)),
            dma((NZ,)), dma((NZ,)), dma((NZ,)), dma((NZ,)),
            dma((NZ,)), dma((NZ,)), dma((NZ,)), dma((NZ,)),
        ],
        compiler_params=pltpu.CompilerParams(
            collective_id=0, has_side_effects=True, vmem_limit_bytes=58 << 20
        ),
    )(activations, out_grads, master, first_moment, second_moment)
    row = jax.ShapeDtypeStruct((ROWS, COLS), f32)
    out = pl.pallas_call(
        finish,
        name="write_out",
        out_shape=(row, row, row, row, jax.ShapeDtypeStruct((NZ, NX, NY, 2, ROWS, COLS), bf16)),
        in_specs=[anywhere, anywhere],
        out_specs=(anywhere,) * 5,
        scratch_shapes=[dma((5,))],
        compiler_params=pltpu.CompilerParams(vmem_limit_bytes=1 << 20),
    )(state, w)
    return out[:4] + (out[4].reshape(D, COLS),)


def solution(mesh):
    spec = P(("dp", "replica"), None)
    return jax.shard_map(
        body, mesh=mesh, in_specs=(spec,) * 5, out_specs=(spec,) * 4 + (P(),), check_vma=False
    )
```
